32 devices in a mesh: row: 4 (over z), col: 8 (over y, x, core).
Axes of the slice: x: 2, y: 2, z: 4, core: 2. Of those that a mesh axis runs over, the one named last changes fastest.
Arguments:
- student_in: bfloat16 [64, 8192], P('col', 'row'), may hold values from -260 to 260
- teacher_hidden: bfloat16 [64, 16384], P(None, 'col'), may hold values from -1600 to 1600
- proj: bfloat16 [16384, 8192], P('col', 'row'), may hold values from -0.046875 to 0.046875
- w_gate: bfloat16 [8192, 28672], P('row', 'col'), may hold values from -0.0625 to 0.0625
- w_up: bfloat16 [8192, 28672], P('row', 'col'), may hold values from -0.0625 to 0.0625
- w_down: bfloat16 [28672, 8192], P('col', 'row'), may hold values from -0.03125 to 0.03125
Outputs:
- grad_gate: bfloat16 [8192, 28672], P('row', 'col')
- grad_up: bfloat16 [8192, 28672], P('row', 'col')
- grad_down: bfloat16 [28672, 8192], P('col', 'row')
- distill_loss: float32 [], replicated
The draws below stay inside these ranges and needn't reach their ends.
All inputs are finite; a program needn't handle non-finite values.
Results may differ from the reference program's by a relative error of at most 0.0099.
Values may be sent and summed in bfloat16 or wider, within the bound.
No kernel may reach another device: no remote copies, remote signals or barrier semaphores. Data moves between devices by JAX's collectives and lax.ppermute only.
A program may use at most 192 MiB of HBM per device.

```python
import jax
import jax.numpy as jnp

D = 8192
FF = 28672
KT = 16384
TOKENS = 64


def draw_student_in(key, part):
    first_key = jax.random.fold_in(key, 11)
    values = jnp.clip(1.5 * jax.random.normal(first_key, (TOKENS, D), jnp.float32), -9.0, 9.0)
    return jnp.clip(values, -260.0, 260.0).astype(jnp.bfloat16)


def draw_teacher_hidden(key, part):
    first_key = jax.random.fold_in(key, 21)
    values = jnp.clip(1.5 * jax.random.normal(first_key, (TOKENS, KT), jnp.float32), -9.0, 9.0)
    return jnp.clip(values, -1600.0, 1600.0).astype(jnp.bfloat16)


def steps_of(key, dims, shards, least, high):
    def one(position, parts):
        steps = jax.random.uniform(jax.random.fold_in(jax.random.fold_in(key, 6), position), (parts,), jnp.float32, least / len(shards), high / len(shards))
        return jnp.repeat(jnp.exp(steps), dims[position] // parts).reshape((-1,) + (1,) * (len(dims) - position - 1))

    factor_of = one(*shards[0])
    for cut in shards[1:]:
        factor_of = factor_of * one(*cut)
    return factor_of


def centred(own_key, extent, scale, bound, pieces=(), dtype=jnp.bfloat16):
    values = scale * jax.random.normal(own_key, extent, jnp.float32)
    if pieces:
        values = values * steps_of(own_key, extent, pieces, -0.22, 0.18)
    return jnp.clip(values, -bound, bound).astype(dtype)


def setup_inputs(seed: int = 0) -> dict:
    keys = jax.random.split(jax.random.key(seed), 7)
    student_in = draw_student_in(jax.random.fold_in(keys[6], 71), 0)
    teacher_hidden = draw_teacher_hidden(jax.random.fold_in(keys[6], 71), 0)
    proj = centred(keys[2], (KT, D), KT ** -0.5, 0.046875, ((0, 8), (1, 4)))
    w_gate = centred(keys[3], (D, FF), D ** -0.5, 0.0625, ((0, 4), (1, 8)))
    w_up = centred(keys[4], (D, FF), D ** -0.5, 0.0625, ((0, 4), (1, 8)))
    w_down = centred(keys[5], (FF, D), FF ** -0.5, 0.03125, ((0, 8), (1, 4)))
    return dict(student_in=student_in, teacher_hidden=teacher_hidden, proj=proj, w_gate=w_gate, w_up=w_up, w_down=w_down)


def reference(student_in, teacher_hidden, proj, w_gate, w_up, w_down):
    gate_val = jnp.dot(student_in, w_gate, preferred_element_type=jnp.float32)
    up_val = jnp.dot(student_in, w_up, preferred_element_type=jnp.float32)
    logistic = jax.nn.sigmoid(gate_val)
    silu_gate = gate_val * logistic
    hidden = (silu_gate * up_val).astype(jnp.bfloat16)
    student = student_in.astype(jnp.float32) + jnp.dot(hidden, w_down, preferred_element_type=jnp.float32)
    teacher = jnp.dot(teacher_hidden, proj, preferred_element_type=jnp.float32)
    log_probs = jax.nn.log_softmax(student, axis=-1)
    target = jax.nn.softmax(teacher, axis=-1)
    distill_loss = jnp.mean(-jnp.sum(target * log_probs, axis=-1))
    stud_grad = (jnp.exp(log_probs) - target).astype(jnp.bfloat16)
    grad_down = jnp.dot(hidden.T, stud_grad, preferred_element_type=jnp.float32).astype(jnp.bfloat16)
    hidden_grad = jnp.dot(stud_grad, w_down.T, preferred_element_type=jnp.float32)
    slope = logistic * (1.0 + gate_val * (1.0 - logistic))
    gate_grad = (hidden_grad * up_val * slope).astype(jnp.bfloat16)
    up_grad = (hidden_grad * silu_gate).astype(jnp.bfloat16)
    grad_gate = jnp.dot(student_in.T, gate_grad, preferred_element_type=jnp.float32).astype(jnp.bfloat16)
    grad_up = jnp.dot(student_in.T, up_grad, preferred_element_type=jnp.float32).astype(jnp.bfloat16)
    return (grad_gate, grad_up, grad_down, distill_loss)
```

```python
import jax
import jax.numpy as jnp
from jax import lax
from jax.experimental import pallas as pl
from jax.experimental.pallas import tpu as pltpu
from jax.sharding import PartitionSpec as P

BF16, F32 = jnp.bfloat16, jnp.float32
MIB = 2**20


def log2(n):
    return n.bit_length() - 1


def swap(value, axis, bit):
    n = lax.axis_size(axis)
    return lax.ppermute(value, axis, [(i, i ^ (1 << bit)) for i in range(n)])


def flip_if(flag, value, axis):
    first, second = jnp.split(value, 2, axis)
    return jnp.where(flag, jnp.concatenate([second, first], axis), value)


def call(kernel, grid, in_specs, out_specs, out_shape, flops, nbytes, aliases=None, vmem=44):
    return pl.pallas_call(
        kernel,
        grid=grid,
        in_specs=in_specs,
        out_specs=out_specs,
        out_shape=out_shape,
        input_output_aliases=aliases or {},
        compiler_params=pltpu.CompilerParams(vmem_limit_bytes=vmem * MIB),
        cost_estimate=pl.CostEstimate(flops=flops, bytes_accessed=nbytes, transcendentals=0),
    )


def whole(shape):
    return pl.BlockSpec(shape, lambda *_: (0,) * len(shape))


def steps_of(width, most):
    for n in range(1, width // 128 + 1):
        if width % (128 * n) == 0 and width // n <= most:
            return n
    return 1


def halves(value, groups):
    rows, width = value.shape
    split = value.reshape(groups, 2, rows // groups // 2, width)
    return split[:, 0].reshape(rows // 2, width), split[:, 1].reshape(rows // 2, width)


def gate_up_chunk(x, w_gate, w_up, k, cw):
    rows, depth = x.shape
    half = rows // 2
    if cw % 128:
        gate = jnp.dot(x, w_gate[:, k * cw : (k + 1) * cw], preferred_element_type=F32)
        up = jnp.dot(x, w_up[:, k * cw : (k + 1) * cw], preferred_element_type=F32)
        (gate_keep, gate_send), (up_keep, up_send) = halves(gate, 2), halves(up, 2)
        return jnp.stack([gate_keep, up_keep]), jnp.stack([gate_send, up_send]).astype(BF16)
    steps = steps_of(cw, 896)
    bn = cw // steps

    def kernel(x_ref, gate_ref, up_ref, keep_ref, send_ref):
        for i, w_ref in enumerate((gate_ref, up_ref)):
            part = jnp.dot(x_ref[...], w_ref[...], preferred_element_type=F32)
            keep, send = halves(part, 2)
            keep_ref[i] = keep
            send_ref[i] = send.astype(BF16)

    wide = pl.BlockSpec((depth, bn), lambda j: (0, k * steps + j))
    out = pl.BlockSpec((2, half, bn), lambda j: (0, 0, j))
    return call(
        kernel,
        (steps,),
        [whole((rows, depth)), wide, wide],
        [out, out],
        [jax.ShapeDtypeStruct((2, half, cw), F32), jax.ShapeDtypeStruct((2, half, cw), BF16)],
        4 * rows * depth * cw,
        4 * depth * cw,
    )(x, w_gate, w_up)


def down_chunk(hidden, w_down, k, before):
    rows, cw = hidden.shape
    width = w_down.shape[1]
    half = rows // 2
    if cw % 128:
        part = jnp.dot(hidden, w_down[k * cw : (k + 1) * cw], preferred_element_type=F32)
        parts = (part[:half], part[half:])
        return parts if before is None else tuple(a + b for a, b in zip(before, parts))
    steps = steps_of(cw, 896)
    bk = cw // steps

    def kernel(h_ref, w_ref, *refs):
        keep_ref, send_ref = refs[-2:]
        j = pl.program_id(0)
        part = jnp.dot(h_ref[...], w_ref[...], preferred_element_type=F32)

        @pl.when(j == 0)
        def _():
            if before is None:
                keep_ref[...] = part[:half]
                send_ref[...] = part[half:]
            else:
                keep_ref[...] = refs[0][...] + part[:half]
                send_ref[...] = refs[1][...] + part[half:]

        @pl.when(j > 0)
        def _():
            keep_ref[...] += part[:half]
            send_ref[...] += part[half:]

    out = whole((half, width))
    shape = jax.ShapeDtypeStruct((half, width), F32)
    return call(
        kernel,
        (steps,),
        [
            pl.BlockSpec((rows, bk), lambda j: (0, j)),
            pl.BlockSpec((bk, width), lambda j: (k * steps + j, 0)),
        ]
        + ([] if before is None else [out, out]),
        [out, out],
        [shape, shape],
        2 * rows * cw * width,
        2 * cw * width,
    )(hidden, w_down, *(before or ()))


def hidden_grad_chunk(stud_grad, w_down, k, cw):
    rows, width = stud_grad.shape
    half = rows // 2
    dims = (((1,), (1,)), ((), ()))
    if cw % 128:
        part = lax.dot_general(
            stud_grad, w_down[k * cw : (k + 1) * cw], dims, preferred_element_type=F32
        )
        keep, send = halves(part, 2)
        return keep, send.astype(BF16)
    steps = steps_of(cw, 896)
    bn = cw // steps

    def kernel(g_ref, w_ref, keep_ref, send_ref):
        part = lax.dot_general(g_ref[...], w_ref[...], dims, preferred_element_type=F32)
        keep, send = halves(part, 2)
        keep_ref[...] = keep
        send_ref[...] = send.astype(BF16)

    out = pl.BlockSpec((half, bn), lambda j: (0, j))
    return call(
        kernel,
        (steps,),
        [whole((rows, width)), pl.BlockSpec((bn, width), lambda j: (k * steps + j, 0))],
        [out, out],
        [jax.ShapeDtypeStruct((half, cw), F32), jax.ShapeDtypeStruct((half, cw), BF16)],
        2 * rows * cw * width,
        2 * cw * width,
    )(stud_grad, w_down)


def outer(left, right):
    dims = (((0,), (0,)), ((), ()))
    return lax.dot_general(left, right, dims, preferred_element_type=F32).astype(BF16)


def weight_grads_chunk(x, hidden_grad, slopes, k, width_ff, before):
    rows, depth = x.shape
    cw = hidden_grad.shape[1]
    if cw % 128:
        return [outer(x, hidden_grad * slopes[i]) for i in (0, 1)]
    bm = min(512, depth)

    def kernel(x_ref, h_ref, s_ref, *refs):
        grad = h_ref[...].astype(F32)
        for i, out_ref in enumerate(refs[-2:]):
            out_ref[...] = outer(x_ref[...], (grad * s_ref[i].astype(F32)).astype(BF16))

    out = pl.BlockSpec((bm, cw), lambda i: (i, k))
    shape = jax.ShapeDtypeStruct((depth, width_ff), BF16)
    prior = [] if before is None else list(before)
    return call(
        kernel,
        (depth // bm,),
        [pl.BlockSpec((rows, bm), lambda i: (0, i)), whole((rows, cw)), whole((2, rows, cw))]
        + [pl.BlockSpec(memory_space=pl.ANY)] * len(prior),
        [out, out],
        [shape, shape],
        4 * rows * depth * cw,
        4 * depth * cw,
        {3: 0, 4: 1} if prior else None,
    )(x, hidden_grad, slopes, *prior)


def down_grad_chunk(hidden, stud_grad, k, width_ff, before):
    rows, cw = hidden.shape
    width = stud_grad.shape[1]
    if cw % 128:
        return outer(hidden, stud_grad)
    steps = steps_of(cw, 896)
    bm = cw // steps

    def kernel(h_ref, g_ref, *refs):
        refs[-1][...] = outer(h_ref[...], g_ref[...])

    prior = [] if before is None else [before]
    return call(
        kernel,
        (steps,),
        [pl.BlockSpec((rows, bm), lambda i: (0, i)), whole((rows, width))]
        + [pl.BlockSpec(memory_space=pl.ANY)] * len(prior),
        pl.BlockSpec((bm, width), lambda i: (k * steps + i, 0)),
        jax.ShapeDtypeStruct((width_ff, width), BF16),
        2 * rows * cw * width,
        2 * cw * width,
        {2: 0} if prior else None,
    )(hidden, stud_grad, *prior)


def local(student_in, teacher_hidden, proj, w_gate, w_up, w_down):
    n_row, n_col = lax.axis_size("row"), lax.axis_size("col")
    row_bits, chip_bits = log2(n_row), log2(n_col) - 1
    row_me, col_me = lax.axis_index("row"), lax.axis_index("col")
    core_me = col_me % 2 == 1
    own, width = student_in.shape
    tokens = own * n_col
    width_ff = w_gate.shape[1]
    chunks = 2 if width_ff % 256 == 0 else 1
    cw = width_ff // chunks
    twos = (2,) * chip_bits

    def row_bit(s):
        return (row_me >> s) % 2 == 1

    teach = teacher_hidden.reshape(*twos, 2, own, -1)
    for s in range(row_bits):
        teach = flip_if(row_bit(s), teach, s)
    teach = jnp.moveaxis(flip_if(core_me, teach, chip_bits), chip_bits, 0)
    teach_part = jnp.dot(teach.reshape(tokens, -1), proj, preferred_element_type=F32)

    x = student_in
    for s in reversed(range(chip_bits)):
        x = jnp.stack([x, swap(x, "col", chip_bits - s)])
    for s in range(chip_bits):
        flag = (col_me >> (chip_bits - s)) % 2 == 1
        if s < row_bits:
            flag = flag ^ row_bit(s)
        x = flip_if(flag, x, s)
    x = x.reshape(tokens // 2, width)
    x = jnp.concatenate([x, swap(x, "col", 0)])

    def reduce_rows(keep, send, lead):
        columns = keep.shape[-1]
        for s in range(row_bits):
            total = keep + swap(send, "row", s).astype(F32)
            if s < row_bits - 1:
                total = total.reshape(lead * 2, 2, -1, columns)
                keep, send = total[:, 0], total[:, 1].astype(BF16)
        return total.reshape(lead, -1, columns)

    def gather_rows(piece, lead):
        columns = piece.shape[-1]
        for s in reversed(range(row_bits)):
            piece = piece.reshape(lead, 2, 1, -1, columns)
            piece = jnp.concatenate([piece, swap(piece, "row", s)], axis=2)
        return piece.reshape(lead, tokens, columns)

    def reduce_cols(keep, send):
        total = keep + swap(send, "col", 0)
        parts = list(jnp.split(total, 2))
        for turn in range(chip_bits):
            for i, bit in enumerate((1 + turn, chip_bits - turn)):
                parts[i] = parts[i] + swap(parts[i], "col", bit)
        return jnp.concatenate(parts)

    def exchange_rows(stats):
        everything = []
        for m in range(n_row):
            if m == 0:
                everything.append(stats)
                continue
            other = lax.ppermute(stats, "row", [(i, i ^ m) for i in range(n_row)])
            other = other.reshape(*twos, own, -1)
            for s in range(row_bits):
                if (m >> s) % 2:
                    first, second = jnp.split(other, 2, s)
                    other = jnp.concatenate([second, first], s)
            everything.append(other.reshape(stats.shape))
        return everything

    def tree_sum(values):
        while len(values) > 1:
            values = [a + b for a, b in zip(values[::2], values[1::2])]
        return values[0]

    hidden, slopes_piece = [], []
    for k in range(chunks):
        keep, send = gate_up_chunk(x, w_gate, w_up, k, cw)
        total = reduce_rows(keep, send, 2)
        gate, up = total[0], total[1]
        logistic = jax.nn.sigmoid(gate)
        silu = gate * logistic
        hidden.append(gather_rows((silu * up).astype(BF16)[None], 1)[0])
        slope = logistic * (1.0 + gate * (1.0 - logistic))
        slopes_piece.append(jnp.stack([up * slope, silu]).astype(BF16))
    slopes = [gather_rows(piece, 2) for piece in slopes_piece]

    teacher = reduce_cols(teach_part[: tokens // 2], teach_part[tokens // 2 :])
    top = jnp.max(teacher, axis=1, keepdims=True)
    norm = jnp.sum(jnp.exp(teacher - top), axis=1, keepdims=True)
    stats = exchange_rows(jnp.concatenate([top, norm], axis=1))
    teach_max = stats[0][:, :1]
    for other in stats[1:]:
        teach_max = jnp.maximum(teach_max, other[:, :1])
    teach_norm = tree_sum([s[:, 1:2] * jnp.exp(s[:, :1] - teach_max) for s in stats])
    target = jnp.exp(teacher - teach_max) / teach_norm

    parts = None
    for k in range(chunks):
        parts = down_chunk(hidden[k], w_down, k, parts)
    student = x[: tokens // 2].astype(F32) + reduce_cols(*parts)
    top = jnp.max(student, axis=1, keepdims=True)
    norm = jnp.sum(jnp.exp(student - top), axis=1, keepdims=True)
    cross = jnp.sum(target * student, axis=1, keepdims=True)
    stats = exchange_rows(jnp.concatenate([top, norm, cross], axis=1))
    stud_max = stats[0][:, :1]
    for other in stats[1:]:
        stud_max = jnp.maximum(stud_max, other[:, :1])
    stud_norm = tree_sum([s[:, 1:2] * jnp.exp(s[:, :1] - stud_max) for s in stats])
    cross = tree_sum([s[:, 2:3] for s in stats])
    own_grad = (jnp.exp(student - stud_max) / stud_norm - target).astype(BF16)
    stud_grad = jnp.concatenate([own_grad, swap(own_grad, "col", 0)])

    token_loss = (stud_max + jnp.log(stud_norm) - cross).reshape(*twos, own)
    for s in range(row_bits):
        token_loss = flip_if(row_bit(s), token_loss, s)
    core_loss = jnp.sum(token_loss.reshape(1, -1), axis=1, keepdims=True)
    distill_loss = ((core_loss + swap(core_loss, "col", 0)) / tokens)[0, 0]

    hidden_grads = []
    for k in range(chunks):
        keep, send = hidden_grad_chunk(stud_grad, w_down, k, cw)
        total = reduce_rows(keep, send, 1)
        hidden_grads.append(gather_rows(total.astype(BF16), 1)[0])
    grad_down = None
    for k in range(chunks):
        grad_down = down_grad_chunk(hidden[k], stud_grad, k, width_ff, grad_down)
    grads = None
    for k in range(chunks):
        grads = weight_grads_chunk(x, hidden_grads[k], slopes[k], k, width_ff, grads)
    return (grads[0], grads[1], grad_down, distill_loss)


def solution(mesh):
    return jax.shard_map(
        local,
        mesh=mesh,
        in_specs=(
            P("col", "row"),
            P(None, "col"),
            P("col", "row"),
            P("row", "col"),
            P("row", "col"),
            P("col", "row"),
        ),
        out_specs=(P("row", "col"), P("row", "col"), P("col", "row"), P()),
        check_vma=False,
    )
```

```python
import jax
import jax.numpy as jnp
from jax import lax
from jax.experimental import pallas as pl
from jax.experimental.pallas import tpu as pltpu
from jax.sharding import PartitionSpec as P

BF16, F32 = jnp.bfloat16, jnp.float32
MIB = 2**20


def log2(n):
    return n.bit_length() - 1


def swap(value, axis, mask):
    return lax.ppermute(value, axis, [(i, i ^ mask) for i in range(lax.axis_size(axis))])


def after(value, others):
    return lax.optimization_barrier((value, others))[0] if jax.tree.leaves(others) else value


VMEM = pl.BlockSpec(memory_space=pltpu.VMEM)


def in_hbm(array):
    return pltpu.with_memory_space_constraint(array, pltpu.HBM)


def spans(start, stop):
    first = min(256, stop - start)
    n = -(-(stop - start - first) // 896)
    cuts = [start, *(start + first + (stop - start - first) * i // (128 * max(n, 1)) * 128 for i in range(n)), stop]
    return list(zip(cuts[:-1], cuts[1:])) if n else [(start, stop)]


def streamed(x, weights, pieces, product, out_shapes, store):
    n = len(pieces)
    shapes = [tuple(cut.stop - cut.start for cut in cuts) for _, cuts in pieces]

    def kernel(x_ref, *refs):
        w_refs, refs = refs[: len(weights)], refs[len(weights) :]
        out_refs, buffers, semaphores = refs[: len(out_shapes)], refs[len(out_shapes) : -1], refs[-1]
        copies = [
            pltpu.make_async_copy(w_refs[which].at[cuts], buffer, semaphores.at[i])
            for i, ((which, cuts), buffer) in enumerate(zip(pieces, buffers))
        ]
        for copy in copies:
            copy.start()
        for i, copy in enumerate(copies):
            copy.wait()
            store(out_refs, i, product(x_ref[...], buffers[i][...]))

    size = sum(a * b for a, b in shapes)
    return pl.pallas_call(
        kernel,
        in_specs=[VMEM] + [pl.BlockSpec(memory_space=pltpu.HBM)] * len(weights),
        out_specs=[VMEM] * len(out_shapes),
        out_shape=out_shapes,
        scratch_shapes=[pltpu.VMEM(shape, BF16) for shape in shapes]
        + [pltpu.SemaphoreType.DMA((n,))],
        compiler_params=pltpu.CompilerParams(vmem_limit_bytes=2 * size + 8 * MIB),
        cost_estimate=pl.CostEstimate(
            flops=2 * x.shape[0] * size, bytes_accessed=2 * size, transcendentals=0
        ),
    )(x, *[in_hbm(w) for w in weights])


def products(x, *weights):
    depth, width = weights[0].shape
    if width % 128:
        return [jnp.dot(x, w, preferred_element_type=F32) for w in weights]
    pieces = []
    for which in range(len(weights)):
        cuts = spans(0, width) if which == 0 else [(at, at + 896) for at in range(0, width, 896)]
        pieces += [(which, (slice(0, depth), slice(at, min(to, width)))) for at, to in cuts]

    def product(left, piece):
        return jnp.dot(left, piece, preferred_element_type=F32)

    def store(refs, n, part):
        which, (_, columns) = pieces[n]
        refs[which][:, columns] = part

    shape = jax.ShapeDtypeStruct((x.shape[0], width), F32)
    return streamed(x, weights, pieces, product, [shape] * len(weights), store)


def fetched(array, tie):
    def kernel(in_ref, out_ref, semaphore):
        copy = pltpu.make_async_copy(in_ref, out_ref, semaphore)
        copy.start()
        copy.wait()

    return pl.pallas_call(
        kernel,
        in_specs=[pl.BlockSpec(memory_space=pltpu.HBM)],
        out_specs=VMEM,
        out_shape=pltpu.VMEM(array.shape, array.dtype),
        scratch_shapes=[pltpu.SemaphoreType.DMA],
        compiler_params=pltpu.CompilerParams(vmem_limit_bytes=20 * MIB),
        cost_estimate=pl.CostEstimate(flops=0, bytes_accessed=2 * array.size, transcendentals=0),
    )(after(array, tie))


def call(kernel, grid, in_specs, out_specs, out_shape, flops, nbytes, aliases=None, vmem=44):
    return pl.pallas_call(
        kernel,
        grid=grid,
        in_specs=in_specs,
        out_specs=out_specs,
        out_shape=out_shape,
        input_output_aliases=aliases or {},
        compiler_params=pltpu.CompilerParams(vmem_limit_bytes=vmem * MIB),
        cost_estimate=pl.CostEstimate(flops=flops, bytes_accessed=nbytes, transcendentals=0),
    )


def whole(array):
    return pl.BlockSpec(array.shape, lambda *_: (0,) * len(array.shape))


def steps_of(width, most):
    for n in range(1, width // 128 + 1):
        if width % (128 * n) == 0 and width // n <= most:
            return n
    return 1


def halves(value, groups):
    rows, width = value.shape
    split = value.reshape(groups, 2, rows // groups // 2, width)
    return split[:, 0].reshape(rows // 2, width), split[:, 1].reshape(rows // 2, width)


def joined(refs):
    return jnp.concatenate([ref[...] for ref in refs])


def outer(left, right):
    dims = (((0,), (0,)), ((), ()))
    return lax.dot_general(left, right, dims, preferred_element_type=F32).astype(BF16)


def down_product(hidden, w_down, groups):
    depth, width = w_down.shape
    rows = sum(piece.shape[0] for piece in hidden)
    if depth % 128:
        return halves(jnp.dot(jnp.concatenate(hidden), w_down, preferred_element_type=F32), groups)
    bn = width // steps_of(width, 512)
    n = len(hidden)

    def kernel(*refs):
        w_ref, out_refs = refs[n], refs[n + 1 :]
        left = joined(refs[:n])
        for at in range(0, width, bn):
            part = jnp.dot(left, w_ref[:, at : at + bn], preferred_element_type=F32)
            for out_ref, half in zip(out_refs, halves(part, groups)):
                out_ref[:, at : at + bn] = half

    shape = jax.ShapeDtypeStruct((rows // 2, width), F32)
    return call(
        kernel,
        (),
        [VMEM] * (n + 1),
        [VMEM] * 2,
        [shape] * 2,
        2 * rows * depth * width,
        2 * depth * width,
        vmem=20,
    )(*hidden, pltpu.with_memory_space_constraint(w_down, pltpu.VMEM))


def hidden_grad_chunk(stud_grad, w_down, k, cw):
    rows, width = stud_grad.shape
    half = rows // 2
    dims = (((1,), (1,)), ((), ()))
    if cw % 128:
        rows_k = w_down[k * cw : (k + 1) * cw]
        part = lax.dot_general(stud_grad, rows_k, dims, preferred_element_type=F32)
        return part[:half], part[half:].astype(BF16)
    start = k * cw
    pieces = [(0, (slice(at, to), slice(0, width))) for at, to in spans(start, start + cw)]

    def product(left, piece):
        return lax.dot_general(left, piece, dims, preferred_element_type=F32)

    def store(refs, n, part):
        rows_n = pieces[n][1][0]
        columns = slice(rows_n.start - start, rows_n.stop - start)
        refs[0][:, columns] = part[:half]
        refs[1][:, columns] = part[half:].astype(BF16)

    shapes = [jax.ShapeDtypeStruct((half, cw), F32), jax.ShapeDtypeStruct((half, cw), BF16)]
    return streamed(stud_grad, [w_down], pieces, product, shapes, store)


def weight_grads_chunk(x, hidden_grad, slopes, k, cw, before):
    rows, depth = x.shape
    width_ff = slopes.shape[2]
    if cw % 128:
        return [outer(x, hidden_grad * slopes[i, :, k * cw : (k + 1) * cw]) for i in (0, 1)]
    bm = min(512, depth)

    def kernel(x_ref, h_ref, s_ref, *refs):
        grad = h_ref[...].astype(F32)
        for i, out_ref in enumerate(refs[-2:]):
            out_ref[...] = outer(x_ref[...], (grad * s_ref[i].astype(F32)).astype(BF16))

    out = pl.BlockSpec((bm, cw), lambda i: (i, k))
    shape = jax.ShapeDtypeStruct((depth, width_ff), BF16)
    prior = [] if before is None else list(before)
    return call(
        kernel,
        (depth // bm,),
        [
            pl.BlockSpec((rows, bm), lambda i: (0, i)),
            whole(hidden_grad),
            pl.BlockSpec((2, rows, cw), lambda i: (0, 0, k)),
        ]
        + [pl.BlockSpec(memory_space=pl.ANY)] * len(prior),
        [out, out],
        [shape, shape],
        4 * rows * depth * cw,
        4 * depth * cw,
        {3: 0, 4: 1} if prior else None,
    )(x, hidden_grad, slopes, *prior)


def down_grad_part(hidden, stud_grad, k, parts, before):
    n, (rows, width) = len(hidden), stud_grad.shape
    width_ff = hidden[0].shape[1]
    if width_ff % 128:
        return outer(jnp.concatenate(hidden), stud_grad)
    bm = width_ff // steps_of(width_ff, 896)
    steps = width_ff // bm // parts

    def kernel(*refs):
        refs[-1][...] = outer(joined(refs[:n]), refs[n][...])

    prior = [] if before is None else [before]
    return call(
        kernel,
        (steps,),
        [pl.BlockSpec((piece.shape[0], bm), lambda i: (0, k * steps + i)) for piece in hidden]
        + [whole(stud_grad)]
        + [pl.BlockSpec(memory_space=pl.ANY)] * len(prior),
        pl.BlockSpec((bm, width), lambda i: (k * steps + i, 0)),
        jax.ShapeDtypeStruct((width_ff, width), BF16),
        2 * rows * width_ff * width // parts,
        2 * width_ff * width // parts,
        {n + 1: 0} if prior else None,
    )(*hidden, stud_grad, *prior)


def local(student_in, teacher_hidden, proj, w_gate, w_up, w_down):
    n_row, n_col = lax.axis_size("row"), lax.axis_size("col")
    n_chip = n_col // 2
    rest = n_chip // n_row
    row_bits, chip_bits = log2(n_row), log2(n_chip)
    row_me, col_me = lax.axis_index("row"), lax.axis_index("col")
    chip_me, core_me = col_me // 2, col_me % 2
    own, width = student_in.shape
    tokens = own * n_col
    width_ff = w_gate.shape[1]
    chunks = 2 if width_ff % 256 == 0 else 1
    cw = width_ff // chunks

    def turned(m):
        return sum(((m >> s) % 2) << (row_bits - 1 - s) for s in range(row_bits))

    def mask(m):
        return turned(m) * rest

    def reorder(rows, chip_mask, core_mask):
        at = jnp.arange(tokens)
        source = (((at // own) ^ (chip_mask * 2 + core_mask)) * own) + at % own
        pick = (source[:, None] == jnp.arange(tokens)[None, :]).astype(BF16)
        return jnp.dot(pick, rows, preferred_element_type=F32).astype(BF16)

    def tree_sum(values):
        while len(values) > 1:
            values = [a + b for a, b in zip(values[::2], values[1::2])]
        return values[0]

    def to_rows(pieces):
        return [swap(pieces[m], "row", m) for m in range(1, n_row)]

    def beside(moved, work):
        return lax.optimization_barrier((moved, work))

    def row_sum(keep, arrived):
        total = keep
        for part in arrived:
            total = total + part.astype(F32)
        return total

    def chip_sum(parts, turn):
        bits = (1 + turn, chip_bits - turn)
        return [part + swap(part, "col", 1 << bit) for part, bit in zip(parts, bits)]

    teacher = reorder(teacher_hidden, mask(row_me), core_me)
    x = student_in
    for s in reversed(range(chip_bits)):
        x, teacher = beside(jnp.stack([x, swap(x, "col", 2 << (chip_bits - 1 - s))]), teacher)
        if s == chip_bits - 1:
            teacher = products(teacher, proj)[0]
    for s in range(chip_bits):
        flag = (chip_me >> (chip_bits - 1 - s)) % 2 == 1
        if s < row_bits:
            flag = flag ^ ((row_me >> s) % 2 == 1)
        first, second = jnp.split(x, 2, s)
        x = jnp.where(flag, jnp.concatenate([second, first], s), x)
    x = x.reshape(n_chip, 1, own, width)
    x = jnp.concatenate([x, swap(x, "col", 1)], axis=1).reshape(tokens, width)
    teacher = halves(teacher, n_chip)
    teacher = teacher[0] + swap(teacher[1], "col", 1)
    x, teacher = beside(x, teacher)

    q = tokens // n_row
    teacher = teacher + swap(teacher, "col", 2)
    both = products(x, w_gate, w_up)
    both, teacher = beside(both, teacher)
    pieces = []
    for m in range(n_row):
        at = turned(m) * q
        pieces.append(jnp.stack([part[at : at + q] for part in both]))
    send = [piece.astype(BF16) for piece in pieces]
    near = fetched(w_down, send[1:]) if width_ff % 128 == 0 else w_down
    arrived, near = beside(to_rows(send), near)
    gate, up = row_sum(pieces[0], arrived)
    logistic = jax.nn.sigmoid(gate)
    silu = gate * logistic
    slope = logistic * (1.0 + gate * (1.0 - logistic))
    slopes = jnp.stack([up * slope, silu]).astype(BF16)
    piece = (silu * up).astype(BF16)
    arrived = to_rows([piece] * n_row)
    teacher = after(teacher, piece)
    for s in range(1, chip_bits):
        teacher = teacher + swap(teacher, "col", 2 << s)
    arrived, teacher = beside(arrived, teacher)
    hidden = [[piece, *arrived][turned(m)] for m in range(n_row)]

    parts = down_product(hidden, near, n_chip)
    parts = jnp.split(parts[0] + swap(parts[1], "col", 1), 2)
    for turn in range(chip_bits):
        parts = chip_sum(parts, turn)
    student = x.reshape(n_chip, 2, own, width)[:, 0].reshape(tokens // 2, width).astype(F32)
    student = student + jnp.concatenate(parts)
    slopes = after(slopes, hidden)
    for s in reversed(range(1, row_bits)):
        slopes = jnp.concatenate([slopes, swap(slopes, "row", 1 << s)], axis=1)
    student, slopes = beside(student, slopes)
    teach_top = jnp.max(teacher, axis=1, keepdims=True)
    teach_exp = jnp.exp(teacher - teach_top)
    teach_norm = jnp.sum(teach_exp, axis=1, keepdims=True)

    top = jnp.max(student, axis=1, keepdims=True)
    stud_exp = jnp.exp(student - top)
    norm = jnp.sum(stud_exp, axis=1, keepdims=True)
    cross = jnp.sum(teach_exp * student, axis=1, keepdims=True)
    own_stats = jnp.concatenate([top, norm, teach_top, teach_norm, cross], axis=1)
    stats = [own_stats]
    for m, other in enumerate(to_rows([own_stats] * n_row), 1):
        other = other.reshape(n_chip, own, -1)
        other = jnp.concatenate([other[j ^ mask(m)] for j in range(n_chip)])
        stats.append(other)

    def merged_max(i):
        most = stats[0][:, i : i + 1]
        for other in stats[1:]:
            most = jnp.maximum(most, other[:, i : i + 1])
        return most, [jnp.exp(s[:, i : i + 1] - most) for s in stats]

    def merged_sum(i, scales):
        return tree_sum([s[:, i : i + 1] * scale for s, scale in zip(stats, scales)])

    stud_max, stud_scales = merged_max(0)
    stud_norm = merged_sum(1, stud_scales)
    _, teach_scales = merged_max(2)
    teach_norm = merged_sum(3, teach_scales)
    cross = merged_sum(4, teach_scales) / teach_norm
    own_grad = stud_exp * (stud_scales[0] / stud_norm) - teach_exp * (teach_scales[0] / teach_norm)
    own_grad = own_grad.astype(BF16)
    pair = [v.reshape(n_chip, 1, own, width) for v in (own_grad, swap(own_grad, "col", 1))]
    stud_grad = jnp.concatenate(pair, axis=1).reshape(tokens, width)

    token_loss = stud_max + jnp.log(stud_norm) - cross
    core_loss = tree_sum([token_loss[j * own : (j + 1) * own] for j in range(n_chip)])
    core_loss = jnp.sum(core_loss, axis=0, keepdims=True)

    last_slopes = swap(after(slopes, own_grad), "row", 1)
    transfers = 2 * row_bits - 1
    keep, send, grad_down, grads, loss = [None] * chunks, [None] * chunks, None, None, core_loss
    for t in range(chunks + transfers):
        active = {k: t - 1 - k for k in range(chunks) if 0 <= t - 1 - k < transfers}
        moved = {k: swap(send[k], "row", 1 << min(i, transfers - 1 - i)) for k, i in active.items()}
        tie = [send[k] for k in active]
        made = {}
        if t < chunks:
            made["parts"] = hidden_grad_chunk(after(stud_grad, tie), w_down, t, cw)
        if t == 1:
            made["slopes"] = jnp.concatenate([slopes, last_slopes], axis=1)
        if 0 <= t - chunks < chunks:
            k = t - chunks
            made["grad_down"] = down_grad_part(after(hidden, tie), stud_grad, k, chunks, grad_down)
        if t == chunks:
            made["loss"] = loss + swap(after(loss, tie), "col", 1)
        if t == chunks + transfers - 1 and chunks > 1:
            made["grads"] = weight_grads_chunk(x, after(send[0], tie), slopes, 0, cw, None)
        moved, made = lax.optimization_barrier((moved, made))
        if "parts" in made:
            keep[t], send[t] = made["parts"]
        slopes, loss = made.get("slopes", slopes), made.get("loss", loss)
        grad_down, grads = made.get("grad_down", grad_down), made.get("grads", grads)
        for k, i in active.items():
            if i < row_bits:
                total = keep[k] + moved[k].astype(F32)
                if i < row_bits - 2:
                    keep[k], send[k] = total[: total.shape[0] // 2], total[total.shape[0] // 2 :].astype(BF16)
                elif i == row_bits - 2:
                    first, second = jnp.split(total.astype(BF16), 2)
                    keep[k], send[k] = total, jnp.concatenate([second, first])
                else:
                    send[k] = total.astype(BF16)
            else:
                send[k] = jnp.concatenate([send[k], moved[k]])
    for k in range(0 if grads is None else 1, chunks):
        grads = weight_grads_chunk(x, send[k], slopes, k, cw, grads)
    return grads[0], grads[1], grad_down, loss[0, 0] / tokens


def solution(mesh):
    return jax.shard_map(
        local,
        mesh=mesh,
        in_specs=(
            P("col", "row"),
            P(None, "col"),
            P("col", "row"),
            P("row", "col"),
            P("row", "col"),
            P("col", "row"),
        ),
        out_specs=(P("row", "col"), P("row", "col"), P("col", "row"), P()),
        check_vma=False,
    )
```

```python
import jax
import jax.numpy as jnp
from jax import lax
from jax.experimental import pallas as pl
from jax.experimental.pallas import tpu as pltpu
from jax.sharding import PartitionSpec as P

BF16, F32 = jnp.bfloat16, jnp.float32
MIB = 2**20


def log2(n):
    return n.bit_length() - 1


def swap(value, axis, mask):
    return lax.ppermute(value, axis, [(i, i ^ mask) for i in range(lax.axis_size(axis))])


def after(value, others):
    return lax.optimization_barrier((value, others))[0] if jax.tree.leaves(others) else value


VMEM = pl.BlockSpec(memory_space=pltpu.VMEM)


def in_hbm(array):
    return pltpu.with_memory_space_constraint(array, pltpu.HBM)


def spans(start, stop):
    first = min(256, stop - start)
    n = -(-(stop - start - first) // 896)
    cuts = [start, *(start + first + (stop - start - first) * i // (128 * max(n, 1)) * 128 for i in range(n)), stop]
    return list(zip(cuts[:-1], cuts[1:])) if n else [(start, stop)]


def streamed(x, weights, pieces, product, out_shapes, store):
    n = len(pieces)
    shapes = [tuple(cut.stop - cut.start for cut in cuts) for _, cuts in pieces]

    def kernel(x_ref, *refs):
        w_refs, refs = refs[: len(weights)], refs[len(weights) :]
        out_refs, buffers, semaphores = refs[: len(out_shapes)], refs[len(out_shapes) : -1], refs[-1]
        copies = [
            pltpu.make_async_copy(w_refs[which].at[cuts], buffer, semaphores.at[i])
            for i, ((which, cuts), buffer) in enumerate(zip(pieces, buffers))
        ]
        for copy in copies:
            copy.start()
        for i, copy in enumerate(copies):
            copy.wait()
            store(out_refs, i, product(x_ref[...], buffers[i][...]))

    size = sum(a * b for a, b in shapes)
    return pl.pallas_call(
        kernel,
        in_specs=[VMEM] + [pl.BlockSpec(memory_space=pltpu.HBM)] * len(weights),
        out_specs=[VMEM] * len(out_shapes),
        out_shape=out_shapes,
        scratch_shapes=[pltpu.VMEM(shape, BF16) for shape in shapes]
        + [pltpu.SemaphoreType.DMA((n,))],
        compiler_params=pltpu.CompilerParams(vmem_limit_bytes=2 * size + 8 * MIB),
        cost_estimate=pl.CostEstimate(
            flops=2 * x.shape[0] * size, bytes_accessed=2 * size, transcendentals=0
        ),
    )(x, *[in_hbm(w) for w in weights])


def products(x, *weights, columns=None):
    depth, width = weights[0].shape
    first, width = columns or (0, width)
    if width % 128:
        return [jnp.dot(x, w[:, first : first + width], preferred_element_type=F32) for w in weights]
    pieces = []
    for which in range(len(weights)):
        cuts = spans(0, width) if which == 0 else [(at, at + 896) for at in range(0, width, 896)]
        pieces += [
            (which, (slice(0, depth), slice(first + at, first + min(to, width)))) for at, to in cuts
        ]

    def product(left, piece):
        return jnp.dot(left, piece, preferred_element_type=F32)

    def store(refs, n, part):
        which, (_, cut) = pieces[n]
        refs[which][:, cut.start - first : cut.stop - first] = part

    shape = jax.ShapeDtypeStruct((x.shape[0], width), F32)
    return streamed(x, weights, pieces, product, [shape] * len(weights), store)


def fetched(array, tie):
    def kernel(in_ref, out_ref, semaphore):
        copy = pltpu.make_async_copy(in_ref, out_ref, semaphore)
        copy.start()
        copy.wait()

    return pl.pallas_call(
        kernel,
        in_specs=[pl.BlockSpec(memory_space=pltpu.HBM)],
        out_specs=VMEM,
        out_shape=pltpu.VMEM(array.shape, array.dtype),
        scratch_shapes=[pltpu.SemaphoreType.DMA],
        compiler_params=pltpu.CompilerParams(vmem_limit_bytes=20 * MIB),
        cost_estimate=pl.CostEstimate(flops=0, bytes_accessed=2 * array.size, transcendentals=0),
    )(after(array, tie))


def call(kernel, grid, in_specs, out_specs, out_shape, flops, nbytes, aliases=None, vmem=44):
    return pl.pallas_call(
        kernel,
        grid=grid,
        in_specs=in_specs,
        out_specs=out_specs,
        out_shape=out_shape,
        input_output_aliases=aliases or {},
        compiler_params=pltpu.CompilerParams(vmem_limit_bytes=vmem * MIB),
        cost_estimate=pl.CostEstimate(flops=flops, bytes_accessed=nbytes, transcendentals=0),
    )


def whole(array):
    return pl.BlockSpec(array.shape, lambda *_: (0,) * len(array.shape))


def steps_of(width, most):
    for n in range(1, width // 128 + 1):
        if width % (128 * n) == 0 and width // n <= most:
            return n
    return 1


def halves(value, groups):
    rows, width = value.shape
    split = value.reshape(groups, 2, rows // groups // 2, width)
    return split[:, 0].reshape(rows // 2, width), split[:, 1].reshape(rows // 2, width)


def joined(refs):
    return jnp.concatenate([ref[...] for ref in refs])


def outer(left, right):
    dims = (((0,), (0,)), ((), ()))
    return lax.dot_general(left, right, dims, preferred_element_type=F32).astype(BF16)


def down_product(hidden, w_down, groups):
    depth, width = w_down.shape
    rows = sum(piece.shape[0] for piece in hidden)
    if depth % 128:
        return halves(jnp.dot(jnp.concatenate(hidden), w_down, preferred_element_type=F32), groups)
    bn = width // steps_of(width, 512)
    n = len(hidden)

    def kernel(*refs):
        w_ref, out_refs = refs[n], refs[n + 1 :]
        left = joined(refs[:n])
        for at in range(0, width, bn):
            part = jnp.dot(left, w_ref[:, at : at + bn], preferred_element_type=F32)
            for out_ref, half in zip(out_refs, halves(part, groups)):
                out_ref[:, at : at + bn] = half

    shape = jax.ShapeDtypeStruct((rows // 2, width), F32)
    return call(
        kernel,
        (),
        [VMEM] * (n + 1),
        [VMEM] * 2,
        [shape] * 2,
        2 * rows * depth * width,
        2 * depth * width,
        vmem=20,
    )(*hidden, pltpu.with_memory_space_constraint(w_down, pltpu.VMEM))


def hidden_grad_chunk(stud_grad, w_down, k, cw):
    rows, width = stud_grad.shape
    half = rows // 2
    dims = (((1,), (1,)), ((), ()))
    if cw % 128:
        rows_k = w_down[k * cw : (k + 1) * cw]
        part = lax.dot_general(stud_grad, rows_k, dims, preferred_element_type=F32)
        return part[:half], part[half:].astype(BF16)
    steps = steps_of(cw, 896)
    bn = cw // steps

    def kernel(g_ref, w_ref, keep_ref, send_ref):
        part = lax.dot_general(g_ref[...], w_ref[...], dims, preferred_element_type=F32)
        keep_ref[...] = part[:half]
        send_ref[...] = part[half:].astype(BF16)

    out = pl.BlockSpec((half, bn), lambda j: (0, j))
    return call(
        kernel,
        (steps,),
        [whole(stud_grad), pl.BlockSpec((bn, width), lambda j: (k * steps + j, 0))],
        [out, out],
        [jax.ShapeDtypeStruct((half, cw), F32), jax.ShapeDtypeStruct((half, cw), BF16)],
        2 * rows * cw * width,
        2 * cw * width,
    )(stud_grad, w_down)


def weight_grads_chunk(x, hidden_grad, slopes, k, cw, before):
    rows, depth = x.shape
    width_ff = slopes.shape[2]
    if cw % 128:
        return [outer(x, hidden_grad * slopes[i, :, k * cw : (k + 1) * cw]) for i in (0, 1)]
    bm = min(512, depth)

    def kernel(x_ref, h_ref, s_ref, *refs):
        grad = h_ref[...].astype(F32)
        for i, out_ref in enumerate(refs[-2:]):
            out_ref[...] = outer(x_ref[...], (grad * s_ref[i].astype(F32)).astype(BF16))

    out = pl.BlockSpec((bm, cw), lambda i: (i, k))
    shape = jax.ShapeDtypeStruct((depth, width_ff), BF16)
    prior = [] if before is None else list(before)
    return call(
        kernel,
        (depth // bm,),
        [
            pl.BlockSpec((rows, bm), lambda i: (0, i)),
            whole(hidden_grad),
            pl.BlockSpec((2, rows, cw), lambda i: (0, 0, k)),
        ]
        + [pl.BlockSpec(memory_space=pl.ANY)] * len(prior),
        [out, out],
        [shape, shape],
        4 * rows * depth * cw,
        4 * depth * cw,
        {3: 0, 4: 1} if prior else None,
    )(x, hidden_grad, slopes, *prior)


def down_grad_part(hidden, stud_grad, k, parts, before):
    n, (rows, width) = len(hidden), stud_grad.shape
    width_ff = hidden[0].shape[1]
    if width_ff % 128:
        return outer(jnp.concatenate(hidden), stud_grad)
    bm = width_ff // steps_of(width_ff, 896)
    steps = width_ff // bm // parts

    def kernel(*refs):
        refs[-1][...] = outer(joined(refs[:n]), refs[n][...])

    prior = [] if before is None else [before]
    return call(
        kernel,
        (steps,),
        [pl.BlockSpec((piece.shape[0], bm), lambda i: (0, k * steps + i)) for piece in hidden]
        + [whole(stud_grad)]
        + [pl.BlockSpec(memory_space=pl.ANY)] * len(prior),
        pl.BlockSpec((bm, width), lambda i: (k * steps + i, 0)),
        jax.ShapeDtypeStruct((width_ff, width), BF16),
        2 * rows * width_ff * width // parts,
        2 * width_ff * width // parts,
        {n + 1: 0} if prior else None,
    )(*hidden, stud_grad, *prior)


def local(student_in, teacher_hidden, proj, w_gate, w_up, w_down):
    n_row, n_col = lax.axis_size("row"), lax.axis_size("col")
    n_chip = n_col // 2
    rest = n_chip // n_row
    row_bits, chip_bits = log2(n_row), log2(n_chip)
    row_me, col_me = lax.axis_index("row"), lax.axis_index("col")
    chip_me, core_me = col_me // 2, col_me % 2
    own, width = student_in.shape
    tokens = own * n_col
    width_ff = w_gate.shape[1]
    chunks = 2 if width_ff % 256 == 0 else 1
    cw = width_ff // chunks

    def turned(m):
        return sum(((m >> s) % 2) << (row_bits - 1 - s) for s in range(row_bits))

    def mask(m):
        return turned(m) * rest

    def reorder(rows, chip_mask, core_mask):
        at = jnp.arange(tokens)
        source = (((at // own) ^ (chip_mask * 2 + core_mask)) * own) + at % own
        pick = (source[:, None] == jnp.arange(tokens)[None, :]).astype(BF16)
        return jnp.dot(pick, rows, preferred_element_type=F32).astype(BF16)

    def tree_sum(values):
        while len(values) > 1:
            values = [a + b for a, b in zip(values[::2], values[1::2])]
        return values[0]

    def to_rows(pieces):
        return [swap(pieces[m], "row", m) for m in range(1, n_row)]

    def beside(moved, work):
        return lax.optimization_barrier((moved, work))

    def row_sum(keep, arrived):
        total = keep
        for part in arrived:
            total = total + part.astype(F32)
        return total

    def chip_sum(parts, turn):
        bits = (1 + turn, chip_bits - turn)
        return [part + swap(part, "col", 1 << bit) for part, bit in zip(parts, bits)]

    teacher = reorder(teacher_hidden, mask(row_me), core_me)
    teacher_parts = []
    x = student_in
    for s in reversed(range(chip_bits)):
        x = jnp.stack([x, swap(x, "col", 2 << (chip_bits - 1 - s))])
        if len(teacher_parts) < 2:
            cut = (len(teacher_parts) * (width // 2), width // 2)
            part = products(after(teacher, teacher_parts), proj, columns=cut)[0]
            x, part = beside(x, part)
            teacher_parts.append(part)
    for s in range(chip_bits):
        flag = (chip_me >> (chip_bits - 1 - s)) % 2 == 1
        if s < row_bits:
            flag = flag ^ ((row_me >> s) % 2 == 1)
        first, second = jnp.split(x, 2, s)
        x = jnp.where(flag, jnp.concatenate([second, first], s), x)
    x = x.reshape(n_chip, 1, own, width)
    x = jnp.concatenate([x, swap(x, "col", 1)], axis=1).reshape(tokens, width)
    teacher = halves(jnp.concatenate(teacher_parts, axis=1), n_chip)
    teacher = teacher[0] + swap(teacher[1], "col", 1)
    x, teacher = beside(x, teacher)

    q = tokens // n_row
    teacher = teacher + swap(teacher, "col", 2)
    both = products(x, w_gate, w_up)
    both, teacher = beside(both, teacher)
    pieces = []
    for m in range(n_row):
        at = turned(m) * q
        pieces.append(jnp.stack([part[at : at + q] for part in both]))
    send = [piece.astype(BF16) for piece in pieces]
    near = fetched(w_down, send[1:]) if width_ff % 128 == 0 else w_down
    arrived, near = beside(to_rows(send), near)
    gate, up = row_sum(pieces[0], arrived)
    logistic = jax.nn.sigmoid(gate)
    silu = gate * logistic
    slope = logistic * (1.0 + gate * (1.0 - logistic))
    slopes = jnp.stack([up * slope, silu]).astype(BF16)
    piece = (silu * up).astype(BF16)
    arrived = to_rows([piece] * n_row)
    teacher = after(teacher, piece)
    for s in range(1, chip_bits):
        teacher = teacher + swap(teacher, "col", 2 << s)
    arrived, teacher = beside(arrived, teacher)
    hidden = [[piece, *arrived][turned(m)] for m in range(n_row)]

    parts = down_product(hidden, near, n_chip)
    parts = jnp.split(parts[0] + swap(parts[1], "col", 1), 2)
    for turn in range(chip_bits):
        parts = chip_sum(parts, turn)
    student = x.reshape(n_chip, 2, own, width)[:, 0].reshape(tokens // 2, width).astype(F32)
    student = student + jnp.concatenate(parts)
    slopes = after(slopes, hidden)
    for s in reversed(range(1, row_bits)):
        slopes = jnp.concatenate([slopes, swap(slopes, "row", 1 << s)], axis=1)
    student, slopes = beside(student, slopes)
    teach_top = jnp.max(teacher, axis=1, keepdims=True)
    teach_exp = jnp.exp(teacher - teach_top)
    teach_norm = jnp.sum(teach_exp, axis=1, keepdims=True)

    top = jnp.max(student, axis=1, keepdims=True)
    stud_exp = jnp.exp(student - top)
    norm = jnp.sum(stud_exp, axis=1, keepdims=True)
    cross = jnp.sum(teach_exp * student, axis=1, keepdims=True)
    own_stats = jnp.concatenate([top, norm, teach_top, teach_norm, cross], axis=1)
    stats = [own_stats]
    for m, other in enumerate(to_rows([own_stats] * n_row), 1):
        other = other.reshape(n_chip, own, -1)
        other = jnp.concatenate([other[j ^ mask(m)] for j in range(n_chip)])
        stats.append(other)

    def merged_max(i):
        most = stats[0][:, i : i + 1]
        for other in stats[1:]:
            most = jnp.maximum(most, other[:, i : i + 1])
        return most, [jnp.exp(s[:, i : i + 1] - most) for s in stats]

    def merged_sum(i, scales):
        return tree_sum([s[:, i : i + 1] * scale for s, scale in zip(stats, scales)])

    stud_max, stud_scales = merged_max(0)
    stud_norm = merged_sum(1, stud_scales)
    _, teach_scales = merged_max(2)
    teach_norm = merged_sum(3, teach_scales)
    cross = merged_sum(4, teach_scales) / teach_norm
    own_grad = stud_exp * (stud_scales[0] / stud_norm) - teach_exp * (teach_scales[0] / teach_norm)
    own_grad = own_grad.astype(BF16)
    pair = [v.reshape(n_chip, 1, own, width) for v in (own_grad, swap(own_grad, "col", 1))]
    stud_grad = jnp.concatenate(pair, axis=1).reshape(tokens, width)

    token_loss = stud_max + jnp.log(stud_norm) - cross
    core_loss = tree_sum([token_loss[j * own : (j + 1) * own] for j in range(n_chip)])
    core_loss = jnp.sum(core_loss, axis=0, keepdims=True)

    last_slopes = swap(after(slopes, own_grad), "row", 1)
    transfers = 2 * row_bits - 1
    keep, send, grad_down, grads, loss = [None] * chunks, [None] * chunks, None, None, core_loss
    for t in range(chunks + transfers):
        active = {k: t - 1 - k for k in range(chunks) if 0 <= t - 1 - k < transfers}
        moved = {k: swap(send[k], "row", 1 << min(i, transfers - 1 - i)) for k, i in active.items()}
        tie = [send[k] for k in active]
        made = {}
        if t < chunks:
            made["parts"] = hidden_grad_chunk(after(stud_grad, tie), w_down, t, cw)
        if t == 1:
            made["slopes"] = jnp.concatenate([slopes, last_slopes], axis=1)
        if 0 <= t - chunks < chunks:
            k = t - chunks
            made["grad_down"] = down_grad_part(after(hidden, tie), stud_grad, k, chunks, grad_down)
        if t == chunks + 1:
            made["loss"] = loss + swap(after(loss, tie), "col", 1)
        if t == chunks + transfers - 1 and chunks > 1:
            made["grads"] = weight_grads_chunk(x, after(send[0], tie), slopes, 0, cw, None)
        moved, made = lax.optimization_barrier((moved, made))
        if "parts" in made:
            keep[t], send[t] = made["parts"]
        slopes, loss = made.get("slopes", slopes), made.get("loss", loss)
        grad_down, grads = made.get("grad_down", grad_down), made.get("grads", grads)
        for k, i in active.items():
            if i < row_bits:
                total = keep[k] + moved[k].astype(F32)
                if i < row_bits - 2:
                    keep[k], send[k] = total[: total.shape[0] // 2], total[total.shape[0] // 2 :].astype(BF16)
                elif i == row_bits - 2:
                    first, second = jnp.split(total.astype(BF16), 2)
                    keep[k], send[k] = total, jnp.concatenate([second, first])
                else:
                    send[k] = total.astype(BF16)
            else:
                send[k] = jnp.concatenate([send[k], moved[k]])
    for k in range(0 if grads is None else 1, chunks):
        grads = weight_grads_chunk(x, send[k], slopes, k, cw, grads)
    return grads[0], grads[1], grad_down, loss[0, 0] / tokens


def solution(mesh):
    return jax.shard_map(
        local,
        mesh=mesh,
        in_specs=(
            P("col", "row"),
            P(None, "col"),
            P("col", "row"),
            P("row", "col"),
            P("row", "col"),
            P("col", "row"),
        ),
        out_specs=(P("row", "col"), P("row", "col"), P("col", "row"), P()),
        check_vma=False,
    )
```

```python
import jax
import jax.numpy as jnp
from jax import lax
from jax.experimental import pallas as pl
from jax.experimental.pallas import tpu as pltpu
from jax.sharding import PartitionSpec as P

BF16, F32 = jnp.bfloat16, jnp.float32
MIB = 2**20


def log2(n):
    return n.bit_length() - 1


def swap(value, axis, mask):
    return lax.ppermute(value, axis, [(i, i ^ mask) for i in range(lax.axis_size(axis))])


def after(value, others):
    return lax.optimization_barrier((value, others))[0] if jax.tree.leaves(others) else value


VMEM = pl.BlockSpec(memory_space=pltpu.VMEM)


def in_hbm(array):
    return pltpu.with_memory_space_constraint(array, pltpu.HBM)


def spans(start, stop):
    first = min(256, stop - start)
    n = -(-(stop - start - first) // 896)
    cuts = [start, *(start + first + (stop - start - first) * i // (128 * max(n, 1)) * 128 for i in range(n)), stop]
    return list(zip(cuts[:-1], cuts[1:])) if n else [(start, stop)]


def streamed(x, weights, pieces, product, out_shapes, store):
    n = len(pieces)
    shapes = [tuple(cut.stop - cut.start for cut in cuts) for _, cuts in pieces]

    def kernel(x_ref, *refs):
        w_refs, refs = refs[: len(weights)], refs[len(weights) :]
        out_refs, buffers, semaphores = refs[: len(out_shapes)], refs[len(out_shapes) : -1], refs[-1]
        copies = [
            pltpu.make_async_copy(w_refs[which].at[cuts], buffer, semaphores.at[i])
            for i, ((which, cuts), buffer) in enumerate(zip(pieces, buffers))
        ]
        for copy in copies:
            copy.start()
        for i, copy in enumerate(copies):
            copy.wait()
            store(out_refs, i, product(x_ref[...], buffers[i][...]))

    size = sum(a * b for a, b in shapes)
    return pl.pallas_call(
        kernel,
        in_specs=[VMEM] + [pl.BlockSpec(memory_space=pltpu.HBM)] * len(weights),
        out_specs=[VMEM] * len(out_shapes),
        out_shape=out_shapes,
        scratch_shapes=[pltpu.VMEM(shape, BF16) for shape in shapes]
        + [pltpu.SemaphoreType.DMA((n,))],
        compiler_params=pltpu.CompilerParams(vmem_limit_bytes=2 * size + 8 * MIB),
        cost_estimate=pl.CostEstimate(
            flops=2 * x.shape[0] * size, bytes_accessed=2 * size, transcendentals=0
        ),
    )(x, *[in_hbm(w) for w in weights])


def products(x, *weights, columns=None):
    depth, width = weights[0].shape
    first, width = columns or (0, width)
    if width % 128:
        return [jnp.dot(x, w[:, first : first + width], preferred_element_type=F32) for w in weights]
    pieces = []
    for which in range(len(weights)):
        cuts = spans(0, width) if which == 0 else [(at, at + 896) for at in range(0, width, 896)]
        pieces += [
            (which, (slice(0, depth), slice(first + at, first + min(to, width)))) for at, to in cuts
        ]

    def product(left, piece):
        return jnp.dot(left, piece, preferred_element_type=F32)

    def store(refs, n, part):
        which, (_, cut) = pieces[n]
        refs[which][:, cut.start - first : cut.stop - first] = part

    shape = jax.ShapeDtypeStruct((x.shape[0], width), F32)
    return streamed(x, weights, pieces, product, [shape] * len(weights), store)


def fetched(array, tie):
    def kernel(in_ref, out_ref, semaphore):
        copy = pltpu.make_async_copy(in_ref, out_ref, semaphore)
        copy.start()
        copy.wait()

    return pl.pallas_call(
        kernel,
        in_specs=[pl.BlockSpec(memory_space=pltpu.HBM)],
        out_specs=VMEM,
        out_shape=pltpu.VMEM(array.shape, array.dtype),
        scratch_shapes=[pltpu.SemaphoreType.DMA],
        compiler_params=pltpu.CompilerParams(vmem_limit_bytes=20 * MIB),
        cost_estimate=pl.CostEstimate(flops=0, bytes_accessed=2 * array.size, transcendentals=0),
    )(after(array, tie))


def call(kernel, grid, in_specs, out_specs, out_shape, flops, nbytes, aliases=None, vmem=44):
    return pl.pallas_call(
        kernel,
        grid=grid,
        in_specs=in_specs,
        out_specs=out_specs,
        out_shape=out_shape,
        input_output_aliases=aliases or {},
        compiler_params=pltpu.CompilerParams(vmem_limit_bytes=vmem * MIB),
        cost_estimate=pl.CostEstimate(flops=flops, bytes_accessed=nbytes, transcendentals=0),
    )


def whole(array):
    return pl.BlockSpec(array.shape, lambda *_: (0,) * len(array.shape))


def steps_of(width, most):
    for n in range(1, width // 128 + 1):
        if width % (128 * n) == 0 and width // n <= most:
            return n
    return 1


def halves(value, groups):
    rows, width = value.shape
    split = value.reshape(groups, 2, rows // groups // 2, width)
    return split[:, 0].reshape(rows // 2, width), split[:, 1].reshape(rows // 2, width)


def joined(refs):
    return jnp.concatenate([ref[...] for ref in refs])


def outer(left, right):
    dims = (((0,), (0,)), ((), ()))
    return lax.dot_general(left, right, dims, preferred_element_type=F32).astype(BF16)


def down_product(hidden, w_down, groups):
    depth, width = w_down.shape
    rows = sum(piece.shape[0] for piece in hidden)
    if depth % 128:
        return halves(jnp.dot(jnp.concatenate(hidden), w_down, preferred_element_type=F32), groups)
    bn = width // steps_of(width, 512)
    n = len(hidden)

    def kernel(*refs):
        w_ref, out_refs = refs[n], refs[n + 1 :]
        left = joined(refs[:n])
        for at in range(0, width, bn):
            part = jnp.dot(left, w_ref[:, at : at + bn], preferred_element_type=F32)
            for out_ref, half in zip(out_refs, halves(part, groups)):
                out_ref[:, at : at + bn] = half

    shape = jax.ShapeDtypeStruct((rows // 2, width), F32)
    return call(
        kernel,
        (),
        [VMEM] * (n + 1),
        [VMEM] * 2,
        [shape] * 2,
        2 * rows * depth * width,
        2 * depth * width,
        vmem=20,
    )(*hidden, pltpu.with_memory_space_constraint(w_down, pltpu.VMEM))


def hidden_grad_chunk(stud_grad, w_down, k, cw):
    rows, width = stud_grad.shape
    half = rows // 2
    dims = (((1,), (1,)), ((), ()))
    if cw % 128:
        rows_k = w_down[k * cw : (k + 1) * cw]
        part = lax.dot_general(stud_grad, rows_k, dims, preferred_element_type=F32)
        return part[:half], part[half:].astype(BF16)
    steps = steps_of(cw, 896)
    bn = cw // steps

    def kernel(g_ref, w_ref, keep_ref, send_ref):
        part = lax.dot_general(g_ref[...], w_ref[...], dims, preferred_element_type=F32)
        keep_ref[...] = part[:half]
        send_ref[...] = part[half:].astype(BF16)

    out = pl.BlockSpec((half, bn), lambda j: (0, j))
    return call(
        kernel,
        (steps,),
        [whole(stud_grad), pl.BlockSpec((bn, width), lambda j: (k * steps + j, 0))],
        [out, out],
        [jax.ShapeDtypeStruct((half, cw), F32), jax.ShapeDtypeStruct((half, cw), BF16)],
        2 * rows * cw * width,
        2 * cw * width,
    )(stud_grad, w_down)


def weight_grads_chunk(x, hidden_grad, slopes, k, cw, before):
    rows, depth = x.shape
    width_ff = slopes.shape[2]
    if cw % 128:
        return [outer(x, hidden_grad * slopes[i, :, k * cw : (k + 1) * cw]) for i in (0, 1)]
    bm = min(512, depth)

    def kernel(x_ref, h_ref, s_ref, *refs):
        grad = h_ref[...].astype(F32)
        for i, out_ref in enumerate(refs[-2:]):
            out_ref[...] = outer(x_ref[...], (grad * s_ref[i].astype(F32)).astype(BF16))

    out = pl.BlockSpec((bm, cw), lambda i: (i, k))
    shape = jax.ShapeDtypeStruct((depth, width_ff), BF16)
    prior = [] if before is None else list(before)
    return call(
        kernel,
        (depth // bm,),
        [
            pl.BlockSpec((rows, bm), lambda i: (0, i)),
            whole(hidden_grad),
            pl.BlockSpec((2, rows, cw), lambda i: (0, 0, k)),
        ]
        + [pl.BlockSpec(memory_space=pl.ANY)] * len(prior),
        [out, out],
        [shape, shape],
        4 * rows * depth * cw,
        4 * depth * cw,
        {3: 0, 4: 1} if prior else None,
    )(x, hidden_grad, slopes, *prior)


def down_grad_part(hidden, stud_grad, k, parts, before):
    n, (rows, width) = len(hidden), stud_grad.shape
    width_ff = hidden[0].shape[1]
    if width_ff % 128:
        return outer(jnp.concatenate(hidden), stud_grad)
    bm = width_ff // steps_of(width_ff, 896)
    steps = width_ff // bm // parts

    def kernel(*refs):
        refs[-1][...] = outer(joined(refs[:n]), refs[n][...])

    prior = [] if before is None else [before]
    return call(
        kernel,
        (steps,),
        [pl.BlockSpec((piece.shape[0], bm), lambda i: (0, k * steps + i)) for piece in hidden]
        + [whole(stud_grad)]
        + [pl.BlockSpec(memory_space=pl.ANY)] * len(prior),
        pl.BlockSpec((bm, width), lambda i: (k * steps + i, 0)),
        jax.ShapeDtypeStruct((width_ff, width), BF16),
        2 * rows * width_ff * width // parts,
        2 * width_ff * width // parts,
        {n + 1: 0} if prior else None,
    )(*hidden, stud_grad, *prior)


def local(student_in, teacher_hidden, proj, w_gate, w_up, w_down):
    n_row, n_col = lax.axis_size("row"), lax.axis_size("col")
    n_chip = n_col // 2
    rest = n_chip // n_row
    row_bits, chip_bits = log2(n_row), log2(n_chip)
    row_me, col_me = lax.axis_index("row"), lax.axis_index("col")
    chip_me, core_me = col_me // 2, col_me % 2
    own, width = student_in.shape
    tokens = own * n_col
    width_ff = w_gate.shape[1]
    chunks = 2 if width_ff % 256 == 0 else 1
    cw = width_ff // chunks

    def turned(m):
        return sum(((m >> s) % 2) << (row_bits - 1 - s) for s in range(row_bits))

    def mask(m):
        return turned(m) * rest

    def reorder(rows, chip_mask, core_mask):
        at = jnp.arange(tokens)
        source = (((at // own) ^ (chip_mask * 2 + core_mask)) * own) + at % own
        pick = (source[:, None] == jnp.arange(tokens)[None, :]).astype(BF16)
        return jnp.dot(pick, rows, preferred_element_type=F32).astype(BF16)

    def tree_sum(values):
        while len(values) > 1:
            values = [a + b for a, b in zip(values[::2], values[1::2])]
        return values[0]

    def to_rows(pieces):
        return [swap(pieces[m], "row", m) for m in range(1, n_row)]

    def beside(moved, work):
        return lax.optimization_barrier((moved, work))

    def row_sum(keep, arrived):
        total = keep
        for part in arrived:
            total = total + part.astype(F32)
        return total

    def chip_sum(parts, turn):
        bits = (1 + turn, chip_bits - turn)
        return [part + swap(part, "col", 1 << bit) for part, bit in zip(parts, bits)]

    teacher = reorder(teacher_hidden, mask(row_me), core_me)
    teacher_parts = []
    x = student_in
    for s in reversed(range(chip_bits)):
        x = jnp.stack([x, swap(x, "col", 2 << (chip_bits - 1 - s))])
        if len(teacher_parts) < 2:
            cut = (len(teacher_parts) * (width // 2), width // 2)
            part = products(after(teacher, teacher_parts), proj, columns=cut)[0]
            x, part = beside(x, part)
            teacher_parts.append(part)
    for s in range(chip_bits):
        flag = (chip_me >> (chip_bits - 1 - s)) % 2 == 1
        if s < row_bits:
            flag = flag ^ ((row_me >> s) % 2 == 1)
        first, second = jnp.split(x, 2, s)
        x = jnp.where(flag, jnp.concatenate([second, first], s), x)
    x = x.reshape(n_chip, 1, own, width)
    x = jnp.concatenate([x, swap(x, "col", 1)], axis=1).reshape(tokens, width)
    teacher = halves(jnp.concatenate(teacher_parts, axis=1), n_chip)
    teacher = teacher[0] + swap(teacher[1], "col", 1)
    x, teacher = beside(x, teacher)

    q = tokens // n_row
    teacher = teacher + swap(teacher, "col", 2)

    def row_pieces(part):
        return [part[turned(m) * q : (turned(m) + 1) * q] for m in range(n_row)]

    gate = row_pieces(products(x, w_gate)[0])
    send = [piece.astype(BF16) for piece in gate]
    up = products(after(x, send), w_up)[0]
    arrived, (up, teacher) = beside(to_rows(send), (up, teacher))
    gate = row_sum(gate[0], arrived)
    up = row_pieces(up)
    send = [piece.astype(BF16) for piece in up]
    near = fetched(w_down, send[1:]) if width_ff % 128 == 0 else w_down
    arrived, near = beside(to_rows(send), near)
    up = row_sum(up[0], arrived)
    logistic = jax.nn.sigmoid(gate)
    silu = gate * logistic
    slope = logistic * (1.0 + gate * (1.0 - logistic))
    slopes = jnp.stack([up * slope, silu]).astype(BF16)
    piece = (silu * up).astype(BF16)
    arrived = to_rows([piece] * n_row)
    teacher = after(teacher, piece)
    for s in range(1, chip_bits):
        teacher = teacher + swap(teacher, "col", 2 << s)
    arrived, teacher = beside(arrived, teacher)
    hidden = [[piece, *arrived][turned(m)] for m in range(n_row)]

    parts = down_product(hidden, near, n_chip)
    parts = jnp.split(parts[0] + swap(parts[1], "col", 1), 2)
    for turn in range(chip_bits):
        parts = chip_sum(parts, turn)
    student = x.reshape(n_chip, 2, own, width)[:, 0].reshape(tokens // 2, width).astype(F32)
    student = student + jnp.concatenate(parts)
    slopes = after(slopes, hidden)
    for s in reversed(range(1, row_bits)):
        slopes = jnp.concatenate([slopes, swap(slopes, "row", 1 << s)], axis=1)
    student, slopes = beside(student, slopes)
    teach_top = jnp.max(teacher, axis=1, keepdims=True)
    teach_exp = jnp.exp(teacher - teach_top)
    teach_norm = jnp.sum(teach_exp, axis=1, keepdims=True)

    top = jnp.max(student, axis=1, keepdims=True)
    stud_exp = jnp.exp(student - top)
    norm = jnp.sum(stud_exp, axis=1, keepdims=True)
    cross = jnp.sum(teach_exp * student, axis=1, keepdims=True)
    own_stats = jnp.concatenate([top, norm, teach_top, teach_norm, cross], axis=1)
    stats = [own_stats]
    for m, other in enumerate(to_rows([own_stats] * n_row), 1):
        other = other.reshape(n_chip, own, -1)
        other = jnp.concatenate([other[j ^ mask(m)] for j in range(n_chip)])
        stats.append(other)

    def merged_max(i):
        most = stats[0][:, i : i + 1]
        for other in stats[1:]:
            most = jnp.maximum(most, other[:, i : i + 1])
        return most, [jnp.exp(s[:, i : i + 1] - most) for s in stats]

    def merged_sum(i, scales):
        return tree_sum([s[:, i : i + 1] * scale for s, scale in zip(stats, scales)])

    stud_max, stud_scales = merged_max(0)
    stud_norm = merged_sum(1, stud_scales)
    _, teach_scales = merged_max(2)
    teach_norm = merged_sum(3, teach_scales)
    cross = merged_sum(4, teach_scales) / teach_norm
    own_grad = stud_exp * (stud_scales[0] / stud_norm) - teach_exp * (teach_scales[0] / teach_norm)
    own_grad = own_grad.astype(BF16)
    pair = [v.reshape(n_chip, 1, own, width) for v in (own_grad, swap(own_grad, "col", 1))]
    stud_grad = jnp.concatenate(pair, axis=1).reshape(tokens, width)

    token_loss = stud_max + jnp.log(stud_norm) - cross
    core_loss = tree_sum([token_loss[j * own : (j + 1) * own] for j in range(n_chip)])
    core_loss = jnp.sum(core_loss, axis=0, keepdims=True)

    last_slopes = swap(after(slopes, own_grad), "row", 1)
    transfers = 2 * row_bits - 1
    keep, send, grad_down, grads, loss = [None] * chunks, [None] * chunks, None, None, core_loss
    for t in range(chunks + transfers):
        active = {k: t - 1 - k for k in range(chunks) if 0 <= t - 1 - k < transfers}
        moved = {k: swap(send[k], "row", 1 << min(i, transfers - 1 - i)) for k, i in active.items()}
        tie = [send[k] for k in active]
        made = {}
        if t < chunks:
            made["parts"] = hidden_grad_chunk(after(stud_grad, tie), w_down, t, cw)
        if t == 1:
            made["slopes"] = jnp.concatenate([slopes, last_slopes], axis=1)
        if 0 <= t - chunks < chunks:
            k = t - chunks
            made["grad_down"] = down_grad_part(after(hidden, tie), stud_grad, k, chunks, grad_down)
        if t == chunks + 1:
            made["loss"] = loss + swap(after(loss, tie), "col", 1)
        if t == chunks + transfers - 1 and chunks > 1:
            made["grads"] = weight_grads_chunk(x, after(send[0], tie), slopes, 0, cw, None)
        moved, made = lax.optimization_barrier((moved, made))
        if "parts" in made:
            keep[t], send[t] = made["parts"]
        slopes, loss = made.get("slopes", slopes), made.get("loss", loss)
        grad_down, grads = made.get("grad_down", grad_down), made.get("grads", grads)
        for k, i in active.items():
            if i < row_bits:
                total = keep[k] + moved[k].astype(F32)
                if i < row_bits - 2:
                    keep[k], send[k] = total[: total.shape[0] // 2], total[total.shape[0] // 2 :].astype(BF16)
                elif i == row_bits - 2:
                    first, second = jnp.split(total.astype(BF16), 2)
                    keep[k], send[k] = total, jnp.concatenate([second, first])
                else:
                    send[k] = total.astype(BF16)
            else:
                send[k] = jnp.concatenate([send[k], moved[k]])
    for k in range(0 if grads is None else 1, chunks):
        grads = weight_grads_chunk(x, send[k], slopes, k, cw, grads)
    return grads[0], grads[1], grad_down, loss[0, 0] / tokens


def solution(mesh):
    return jax.shard_map(
        local,
        mesh=mesh,
        in_specs=(
            P("col", "row"),
            P(None, "col"),
            P("col", "row"),
            P("row", "col"),
            P("row", "col"),
            P("col", "row"),
        ),
        out_specs=(P("row", "col"), P("row", "col"), P("col", "row"), P()),
        check_vma=False,
    )
```
